256 devices in a mesh: head: 4 (over x_lo, core), seq: 64 (over z, y, x_hi).
Axes of the slice: x: 4 (x_hi: 2, x_lo: 2; x = x_hi * 2 + x_lo), y: 4, z: 8, core: 2. Of those that a mesh axis runs over, the one named last changes fastest.
Arguments:
- query: float32 [32768, 2048], P(('seq', 'head')), may hold values from -8 to 8
- key_in: float32 [32768, 1024], P(('seq', 'head')), may hold values from -8 to 8
- value_in: float32 [32768, 1024], P(('seq', 'head')), may hold values from -6 to 6
- d_out: float32 [32768, 2048], P(('seq', 'head')), may hold values from -48 to 48
Outputs:
- grad_query: float32 [32768, 2048], P(('seq', 'head'))
- grad_key: float32 [32768, 1024], P(('seq', 'head'))
- grad_value: float32 [32768, 1024], P(('seq', 'head'))
The draws below stay inside these ranges and needn't reach their ends.
All inputs are finite; a program needn't handle non-finite values.
Results may differ from the reference program's by a relative error of at most 0.00045.
Values sent between devices are 32-bit elements; how exact they have to be, the bound alone decides.
A program may use at most 64 MiB of HBM per device.

```python
import jax
import jax.numpy as jnp
from jax import lax

HD = 128
QHEADS = 16
KVHEADS = 8
TOK_DEV = 512
WINDOW = 1024
TOKENS = 32768
N_SEQ = 64


def draw_query(key, part):
    base = jax.random.normal(jax.random.fold_in(key, 11), (TOKENS, QHEADS * HD), jnp.float32)
    return jnp.clip(base, -8.0, 8.0)


def draw_key_in(key, part):
    base = jax.random.normal(jax.random.fold_in(key, 12), (TOKENS, KVHEADS * HD), jnp.float32)
    return jnp.clip(base, -8.0, 8.0)


def steps_of(rng, dims, cuts, least, high):
    level = 1.0
    for position, parts in cuts:
        draws = jax.random.uniform(jax.random.fold_in(jax.random.fold_in(rng, 6), position), (parts,), jnp.float32, least / len(cuts), high / len(cuts))
        level = level * jnp.repeat(jnp.exp(draws), dims[position] // parts).reshape((-1,) + (1,) * (len(dims) - 1 - position))
    return level


def centred(own_key, dims, spread, most, split=(), kind=jnp.bfloat16):
    result = jax.random.normal(own_key, dims, jnp.float32) * spread
    if len(split) > 0:
        result = steps_of(own_key, dims, split, -0.22, 0.18) * result
    return jnp.clip(result, min=-most, max=most).astype(kind)


def setup_inputs(seed: int = 0) -> dict:
    arg_keys = jax.random.split(jax.random.key(seed), 5)
    return {
        "query": draw_query(jax.random.fold_in(arg_keys[4], 71), 0),
        "key_in": draw_key_in(jax.random.fold_in(arg_keys[4], 71), 0),
        "value_in": centred(arg_keys[2], (TOKENS, KVHEADS * HD), 1.0, 6.0, ((0, 256),), jnp.float32),
        "d_out": centred(arg_keys[3], (TOKENS, QHEADS * HD), 8.0, 48.0, ((0, 256),), jnp.float32),
    }


score_scale = 168.0 ** -0.5
highest = lax.Precision.HIGHEST


def band_grads(query_block, key_block, value_block, grad_block, start, reach):
    shard_rows = query_block.shape[0]
    key_rows = key_block.shape[0]
    group_size = query_block.shape[1] // key_block.shape[1]
    query_heads = query_block.reshape(shard_rows, -1, group_size, HD)
    grad_heads = grad_block.reshape(shard_rows, -1, group_size, HD)
    key_heads = key_block.reshape(key_rows, -1, HD)
    value_heads = value_block.reshape(key_rows, -1, HD)
    scores = jnp.einsum("qkgd,pkd->kgqp", query_heads, key_heads, precision=highest) * score_scale
    query_index = start + jnp.arange(shard_rows, dtype=jnp.int32)[:, None]
    key_index = start - 2 * shard_rows + jnp.arange(key_rows, dtype=jnp.int32)[None, :]
    inside = (key_index <= query_index) & (key_index > query_index - reach) & (key_index >= 0)
    scores = jnp.where(inside, scores, -jnp.inf)
    highest_score = jnp.max(scores, axis=-1, keepdims=True)
    raised = jnp.exp(scores - highest_score)
    weights = raised / jnp.sum(raised, axis=-1, keepdims=True)
    output = jnp.einsum("kgqp,pkd->qkgd", weights, value_heads, precision=highest)
    row_dot = jnp.einsum("qkgd,qkgd->kgq", grad_heads, output, precision=highest)
    grad_weight = jnp.einsum("qkgd,pkd->kgqp", grad_heads, value_heads, precision=highest)
    grad_score = weights * (grad_weight - row_dot[..., None])
    grad_query = jnp.einsum("kgqp,pkd->qkgd", grad_score, key_heads, precision=highest) * score_scale
    grad_key = jnp.einsum("kgqp,qkgd->pkd", grad_score, query_heads, precision=highest) * score_scale
    grad_value = jnp.einsum("kgqp,qkgd->pkd", weights, grad_heads, precision=highest)
    return (grad_query.reshape(shard_rows, -1), grad_key.reshape(key_rows, -1), grad_value.reshape(key_rows, -1))


def reference(query, key_in, value_in, d_out):
    shard_rows = TOK_DEV
    front = jnp.zeros((2 * shard_rows, key_in.shape[1]), jnp.float32)
    key_padded = jnp.concatenate([front, key_in], axis=0)
    value_padded = jnp.concatenate([front, value_in], axis=0)

    def step(totals, block_id):
        key_total, value_total = totals
        start = block_id * shard_rows
        query_block = lax.dynamic_slice_in_dim(query, start, shard_rows, 0)
        grad_block = lax.dynamic_slice_in_dim(d_out, start, shard_rows, 0)
        key_block = lax.dynamic_slice_in_dim(key_padded, start, 3 * shard_rows, 0)
        value_block = lax.dynamic_slice_in_dim(value_padded, start, 3 * shard_rows, 0)
        grad_query, grad_key, grad_value = band_grads(query_block, key_block, value_block, grad_block, start, WINDOW)
        key_total = lax.dynamic_update_slice_in_dim(key_total, lax.dynamic_slice_in_dim(key_total, start, 3 * shard_rows, 0) + grad_key, start, 0)
        value_total = lax.dynamic_update_slice_in_dim(value_total, lax.dynamic_slice_in_dim(value_total, start, 3 * shard_rows, 0) + grad_value, start, 0)
        return (key_total, value_total), grad_query

    init = (jnp.zeros_like(key_padded), jnp.zeros_like(value_padded))
    (key_total, value_total), query_parts = lax.scan(step, init, jnp.arange(N_SEQ, dtype=jnp.int32))
    return (query_parts.reshape(TOKENS, -1), key_total[2 * shard_rows:], value_total[2 * shard_rows:])
```

```python
import math

import jax
import jax.numpy as jnp
from jax import lax
from jax.experimental import pallas as pl
from jax.experimental.pallas import tpu as pltpu
from jax.sharding import PartitionSpec as P

HD = 128
TOK = 128
RING = 8
TILE = 256
TILES = 4
SPAN = TILES + 1
CHUNK = 64
LOG2E = math.log2(math.e)
LN2 = math.log(2.0)
score_scale = 168.0 ** (-0.5)
MESH = pl.DeviceIdType.MESH
f32 = jnp.float32
bf16 = jnp.bfloat16


def halves(value):
    high = value.astype(bf16)
    low = (value - high.astype(f32)).astype(bf16)
    return high, low


def dot_nt(a, b):
    return lax.dot_general(a, b, (((1,), (1,)), ((), ())), preferred_element_type=f32)


def dot_nn(a, b):
    return lax.dot_general(a, b, (((1,), (0,)), ((), ())), preferred_element_type=f32)


def kernel(
    rows,
    q_in, k_in, v_in, g_in,
    dq_out, dk_out, dv_out,
    kst, vst, qst, gst,
    k4, v4, kt, q4, q2, g4, g2,
    sbuf, pbuf, wcat, scat, scol,
    dkacc, dvacc, dqst, hk, hv, dkf, dvf,
    k_send, k_recv, v_send, v_recv, q_send, q_recv, g_send, g_recv,
    pk_send, pk_recv, pv_send, pv_recv,
    hk_send, hk_recv, hv_send, hv_recv,
    dq_send, dq_recv, dk_send, dk_recv, dv_send, dv_recv,
):
    seq = lax.axis_index("seq")
    head = lax.axis_index("head")
    row = seq // 2
    me = lax.rem(seq, 2) * 4 + head
    chip = me // 2
    core = lax.rem(me, 2)
    has_prev = row > 0
    has_next = row < rows - 1

    def device(r, p):
        return {"seq": 2 * r + p // 4, "head": lax.rem(p, 4)}

    def peer(i, sign):
        j = i // 2
        step = 3 if j == 2 else 2 if j == 3 else j
        return lax.rem(chip + 4 + sign * step, 4) * 2 + lax.rem(core + i % 2, 2)

    def source(i):
        j = i // 2
        step = jnp.where(j == 2, 3, jnp.where(j == 3, 2, j))
        return lax.rem(chip + 4 - step, 4) * 2 + lax.rem(core + lax.rem(i, 2), 2)

    def remote(src, dst, send, recv, r, p):
        return pltpu.make_async_remote_copy(
            src_ref=src, dst_ref=dst, send_sem=send, recv_sem=recv,
            device_id=device(r, p), device_id_type=MESH,
        )

    barrier = pltpu.get_barrier_semaphore()
    for i in range(1, RING):
        pl.semaphore_signal(barrier, inc=1, device_id=device(row, peer(i, 1)), device_id_type=MESH)

    @pl.when(has_prev)
    def _():
        pl.semaphore_signal(barrier, inc=1, device_id=device(row - 1, me), device_id_type=MESH)

    @pl.when(has_next)
    def _():
        pl.semaphore_signal(barrier, inc=1, device_id=device(row + 1, me), device_id_type=MESH)

    pl.semaphore_wait(barrier, RING - 1 + has_prev.astype(jnp.int32) + has_next.astype(jnp.int32))

    def columns(p, width):
        return pl.ds(pl.multiple_of(p * width, width), width)

    for src, width, stage, send, recv, first in (
        (k_in, HD, kst, k_send, k_recv, RING),
        (v_in, HD, vst, v_send, v_recv, RING),
        (q_in, 2 * HD, qst, q_send, q_recv, 0),
        (g_in, 2 * HD, gst, g_send, g_recv, 0),
    ):
        pltpu.make_async_copy(
            src.at[:, columns(me, width)], stage.at[first + me], recv.at[me]
        ).start()
    for pair in (
        ((k_in, HD, kst, k_send, k_recv, RING), (v_in, HD, vst, v_send, v_recv, RING)),
        ((q_in, 2 * HD, qst, q_send, q_recv, 0), (g_in, 2 * HD, gst, g_send, g_recv, 0)),
    ):
        for i in range(1, RING):
            for src, width, stage, send, recv, first in pair:
                to = peer(i, 1)
                remote(
                    src.at[:, columns(to, width)], stage.at[first + me],
                    send.at[to], recv.at[me], row, to,
                ).start()

    dkacc[...] = jnp.zeros_like(dkacc)
    dvacc[...] = jnp.zeros_like(dvacc)

    def landed(ref, sem):
        pltpu.make_async_copy(ref, ref, sem).wait()

    def prepare(block):
        at = pl.ds(pl.multiple_of(block * TOK, TOK), TOK)
        key = kst[block]
        high, low = halves(key)
        k4[at, :] = jnp.concatenate([high, low, high, low], axis=1)
        high, low = halves(key.T)
        kt[:, at] = jnp.concatenate([high, low], axis=0)
        high, low = halves(vst[block])
        v4[at, :] = jnp.concatenate([high, low, high, low], axis=1)

    def own_block(i, carry):
        p = source(i)
        landed(kst.at[RING + p], k_recv.at[p])
        landed(vst.at[RING + p], v_recv.at[p])

        @pl.when(has_next)
        def _():
            remote(kst.at[RING + p], kst.at[p], pk_send.at[p], pk_recv.at[p], row + 1, me).start()
            remote(vst.at[RING + p], vst.at[p], pv_send.at[p], pv_recv.at[p], row + 1, me).start()

        prepare(RING + p)
        return carry

    lax.fori_loop(0, RING, own_block, 0)

    @pl.when(has_prev)
    def _():
        def prev_block(i, carry):
            p = source(i)
            landed(kst.at[p], pk_recv.at[p])
            landed(vst.at[p], pv_recv.at[p])
            prepare(p)
            return carry

        lax.fori_loop(0, RING, prev_block, 0)

    @pl.when(jnp.logical_not(has_prev))
    def _():
        k4[: RING * TOK, :] = jnp.zeros((RING * TOK, 4 * HD), bf16)
        v4[: RING * TOK, :] = jnp.zeros((RING * TOK, 4 * HD), bf16)
        kt[:, : RING * TOK] = jnp.zeros((2 * HD, RING * TOK), bf16)

    lanes = 2 * TILE

    def query_tile(b):
        for e in range(2):
            landed(qst.at[2 * b + e], q_recv.at[2 * b + e])
            landed(gst.at[2 * b + e], g_recv.at[2 * b + e])
        for e in range(2):
            for h in range(2):
                at = slice(h * TILE + e * TOK, h * TILE + (e + 1) * TOK)
                at2 = slice(lanes + h * TILE + e * TOK, lanes + h * TILE + (e + 1) * TOK)
                cols = slice(h * HD, (h + 1) * HD)
                high, low = halves(qst[2 * b + e, :, cols] * (score_scale * LOG2E))
                q4[at, :] = jnp.concatenate([high, high, low, low], axis=1)
                both = jnp.concatenate([high, low], axis=1)
                q2[at, :] = both
                q2[at2, :] = both
                high, low = halves(gst[2 * b + e, :, cols])
                g4[at, :] = jnp.concatenate([high, high, low, low], axis=1)
                both = jnp.concatenate([high, low], axis=1)
                g2[at, :] = both
                g2[at2, :] = both

        def keys(j):
            return pl.ds(pl.multiple_of((b + j) * TILE, TILE), TILE)

        top = jnp.full((8, lanes), -1e30, f32)
        for j in range(SPAN):
            score = dot_nt(k4[keys(j), :], q4[...])
            if j in (0, SPAN - 1):
                key = lax.broadcasted_iota(jnp.int32, (TILE, lanes), 0)
                query = lax.broadcasted_iota(jnp.int32, (TILE, lanes), 1) & (TILE - 1)
                score = jnp.where(key > query if j == 0 else key <= query, score, -1e30)
            if j < SPAN - 1:
                absent = jnp.logical_and(jnp.logical_not(has_prev), b + j < TILES)
                score = score + jnp.where(absent, -1e30, 0.0)
            sbuf[j * TILE : (j + 1) * TILE, :] = score
            top = jnp.maximum(top, jnp.max(score.reshape(TILE // 8, 8, lanes), axis=0))
            pbuf[j * TILE : (j + 1) * TILE, :] = dot_nt(v4[keys(j), :], g4[...])
        top = jnp.max(top, axis=0, keepdims=True)
        total = jnp.zeros((8, lanes), f32)
        inner = jnp.zeros((8, lanes), f32)
        for n in range(SPAN * TILE // CHUNK):
            at = slice(n * CHUNK, (n + 1) * CHUNK)
            raised = jnp.exp2(sbuf[at, :] - top)
            sbuf[at, :] = raised
            total = total + jnp.sum(raised.reshape(CHUNK // 8, 8, lanes), axis=0)
            inner = inner + jnp.sum((raised * pbuf[at, :]).reshape(CHUNK // 8, 8, lanes), axis=0)
        inverse = 1.0 / jnp.sum(total, axis=0, keepdims=True)
        inner = jnp.sum(inner, axis=0, keepdims=True) * inverse
        turned = jnp.zeros((2 * HD, lanes), f32)
        for j in range(SPAN):
            for n in range(TILE // CHUNK):
                at = slice(j * TILE + n * CHUNK, j * TILE + (n + 1) * CHUNK)
                to = slice(n * CHUNK, (n + 1) * CHUNK)
                weight = sbuf[at, :] * inverse
                slope = weight * (pbuf[at, :] - inner)
                high, low = halves(weight)
                wcat[j % 2, to, :lanes] = high
                wcat[j % 2, to, lanes:] = low
                high, low = halves(slope)
                scat[j % 2, to, :lanes] = high
                scat[j % 2, to, lanes:] = low
            part = dot_nn(wcat[j % 2], g2[...])
            dvacc[keys(j), :] += part[:, :HD] + part[:, HD:]
            part = dot_nn(scat[j % 2], q2[...])
            dkacc[keys(j), :] += part[:, :HD] + part[:, HD:]
            turned = turned + dot_nn(kt[:, keys(j)], scat[j % 2, :, :lanes])
            turned = turned + dot_nn(kt[:, keys(j)], scat[j % 2, :, lanes:])
        grad = (turned[:HD] + turned[HD:]) * score_scale
        for e in range(2):
            to = 2 * b + e
            for h in range(2):
                part = grad[:, h * TILE + e * TOK : h * TILE + (e + 1) * TOK]
                dqst[to, :, h * HD : (h + 1) * HD] = part.T

            @pl.when(to == me)
            def _():
                pltpu.make_async_copy(dqst.at[to], dq_out.at[:, columns(me, 2 * HD)], dq_recv.at[me]).start()

            @pl.when(to != me)
            def _():
                remote(
                    dqst.at[to], dq_out.at[:, columns(me, 2 * HD)],
                    dq_send.at[to], dq_recv.at[me], row, to,
                ).start()

    def tile_rows(t):
        return pl.ds(pl.multiple_of(t * TILE, TILE), TILE)

    def send_back(t):
        @pl.when(has_prev)
        def _():
            remote(dkacc.at[tile_rows(t)], hk.at[t], hk_send.at[t], hk_recv.at[t], row - 1, me).start()
            remote(dvacc.at[tile_rows(t)], hv.at[t], hv_send.at[t], hv_recv.at[t], row - 1, me).start()

    def step(i, carry):
        b = jnp.where(i == 0, chip, jnp.where(i <= chip, i - 1, i))
        query_tile(b)
        for t in range(TILES):
            ready = jnp.where(t < chip, t + 1, t)

            @pl.when(i == ready)
            def _():
                send_back(t)
        return carry

    lax.fori_loop(0, TILES, step, 0)

    def finish(t, carry):
        @pl.when(has_next)
        def _():
            landed(hk.at[t], hk_recv.at[t])
            landed(hv.at[t], hv_recv.at[t])

        @pl.when(jnp.logical_not(has_next))
        def _():
            hk[t] = jnp.zeros((TILE, HD), f32)
            hv[t] = jnp.zeros((TILE, HD), f32)

        own = pl.ds(pl.multiple_of(RING * TOK + t * TILE, TILE), TILE)
        dkf[t] = (dkacc[own, :] + hk[t]) * LN2
        dvf[t] = dvacc[own, :] + hv[t]
        for e in range(2):
            to = 2 * t + e
            part = slice(e * TOK, (e + 1) * TOK)

            @pl.when(to == me)
            def _():
                pltpu.make_async_copy(dkf.at[t, part], dk_out.at[:, columns(me, HD)], dk_recv.at[me]).start()
                pltpu.make_async_copy(dvf.at[t, part], dv_out.at[:, columns(me, HD)], dv_recv.at[me]).start()

            @pl.when(to != me)
            def _():
                remote(dkf.at[t, part], dk_out.at[:, columns(me, HD)], dk_send.at[to], dk_recv.at[me], row, to).start()
                remote(dvf.at[t, part], dv_out.at[:, columns(me, HD)], dv_send.at[to], dv_recv.at[me], row, to).start()
        return carry

    lax.fori_loop(0, TILES, finish, 0)

    def sent(p, carry):
        @pl.when(p != me)
        def _():
            landed(kst.at[RING + me], k_send.at[p])
            landed(vst.at[RING + me], v_send.at[p])
            landed(qst.at[me], q_send.at[p])
            landed(gst.at[me], g_send.at[p])
            landed(dqst.at[p], dq_send.at[p])
            landed(dkf.at[0, :TOK], dk_send.at[p])
            landed(dvf.at[0, :TOK], dv_send.at[p])

        @pl.when(has_next)
        def _():
            landed(kst.at[RING + p], pk_send.at[p])
            landed(vst.at[RING + p], pv_send.at[p])

        return carry

    lax.fori_loop(0, RING, sent, 0)

    @pl.when(has_prev)
    def _():
        def halo_sent(t, carry):
            landed(dkacc.at[tile_rows(t)], hk_send.at[t])
            landed(dvacc.at[tile_rows(t)], hv_send.at[t])
            return carry

        lax.fori_loop(0, TILES, halo_sent, 0)

    def got(p, carry):
        landed(dq_out.at[:, columns(p, 2 * HD)], dq_recv.at[p])
        landed(dk_out.at[:, columns(p, HD)], dk_recv.at[p])
        landed(dv_out.at[:, columns(p, HD)], dv_recv.at[p])
        return carry

    lax.fori_loop(0, RING, got, 0)


def solution(mesh):
    rows = mesh.shape["seq"] // 2

    def per_device(query, key_in, value_in, d_out):
        lanes = 2 * TILE
        all_keys = 2 * RING * TOK
        dma = pltpu.SemaphoreType.DMA
        return pl.pallas_call(
            lambda *refs: kernel(rows, *refs),
            out_shape=(
                jax.ShapeDtypeStruct(query.shape, f32),
                jax.ShapeDtypeStruct(key_in.shape, f32),
                jax.ShapeDtypeStruct(value_in.shape, f32),
            ),
            in_specs=[pl.BlockSpec(memory_space=pl.ANY)] * 4,
            out_specs=[pl.BlockSpec(memory_space=pl.ANY)] * 3,
            scratch_shapes=[
                pltpu.VMEM((2 * RING, TOK, HD), f32),
                pltpu.VMEM((2 * RING, TOK, HD), f32),
                pltpu.VMEM((RING, TOK, 2 * HD), f32),
                pltpu.VMEM((RING, TOK, 2 * HD), f32),
                pltpu.VMEM((all_keys, 4 * HD), bf16),
                pltpu.VMEM((all_keys, 4 * HD), bf16),
                pltpu.VMEM((2 * HD, all_keys), bf16),
                pltpu.VMEM((lanes, 4 * HD), bf16),
                pltpu.VMEM((2 * lanes, 2 * HD), bf16),
                pltpu.VMEM((lanes, 4 * HD), bf16),
                pltpu.VMEM((2 * lanes, 2 * HD), bf16),
                pltpu.VMEM((SPAN * TILE, lanes), f32),
                pltpu.VMEM((SPAN * TILE, lanes), f32),
                pltpu.VMEM((2, TILE, 2 * lanes), bf16),
                pltpu.VMEM((2, TILE, 2 * lanes), bf16),
                pltpu.VMEM((8, 128), f32),
                pltpu.VMEM((all_keys, HD), f32),
                pltpu.VMEM((all_keys, HD), f32),
                pltpu.VMEM((RING, TOK, 2 * HD), f32),
                pltpu.VMEM((TILES, TILE, HD), f32),
                pltpu.VMEM((TILES, TILE, HD), f32),
                pltpu.VMEM((TILES, TILE, HD), f32),
                pltpu.VMEM((TILES, TILE, HD), f32),
            ]
            + [dma((RING,))] * 12
            + [dma((TILES,))] * 4
            + [dma((RING,))] * 6,
            compiler_params=pltpu.CompilerParams(
                collective_id=0, has_side_effects=True, vmem_limit_bytes=48 * 2**20
            ),
            cost_estimate=pl.CostEstimate(
                flops=5 * 2 * 2 * 1024 * 1280 * HD, bytes_accessed=6 * 2**20, transcendentals=2 * 1024 * 1280
            ),
        )(query, key_in, value_in, d_out)

    spec = P(("seq", "head"), None)
    return jax.shard_map(
        per_device, mesh=mesh, in_specs=(spec,) * 4, out_specs=(spec,) * 3, check_vma=False
    )
```

```python
import math

import jax
import jax.numpy as jnp
from jax import lax
from jax.experimental import pallas as pl
from jax.experimental.pallas import tpu as pltpu
from jax.sharding import PartitionSpec as P

HD = 128
TOK = 128
RING = 8
TILE = 256
TILES = 4
SPAN = TILES + 1
CHUNK = 64
LOG2E = math.log2(math.e)
LN2 = math.log(2.0)
ORDER = ((0, 1, 3, 2), (1, 0, 2, 3), (2, 0, 1, 3), (3, 0, 2, 1))
score_scale = 168.0 ** (-0.5)
MESH = pl.DeviceIdType.MESH
f32 = jnp.float32
bf16 = jnp.bfloat16


def halves(value):
    high = value.astype(bf16)
    low = (value - high.astype(f32)).astype(bf16)
    return high, low


def dot_nt(a, b):
    return lax.dot_general(a, b, (((1,), (1,)), ((), ())), preferred_element_type=f32)


def dot_nn(a, b):
    return lax.dot_general(a, b, (((1,), (0,)), ((), ())), preferred_element_type=f32)


def kernel(
    rows,
    q_in, k_in, v_in, g_in,
    dq_out, dk_out, dv_out,
    kst, vst, qst, gst,
    k4, v4, kt, q4, q2, g4, g2,
    sbuf, pbuf, wcat, scat,
    dkacc, dvacc, dqst, hk, hv, dkf, dvf,
    k_send, k_recv, v_send, v_recv, q_send, q_recv, g_send, g_recv,
    pk_send, pk_recv, pv_send, pv_recv,
    hk_send, hk_recv, hv_send, hv_recv,
    dq_send, dq_recv, dk_send, dk_recv, dv_send, dv_recv,
):
    seq = lax.axis_index("seq")
    head = lax.axis_index("head")
    row = seq // 2
    me = lax.rem(seq, 2) * 4 + head
    chip = me // 2
    core = lax.rem(me, 2)
    has_prev = row > 0
    has_next = row < rows - 1

    def by_chip(table):
        lines = [sum(n << (2 * k) for k, n in enumerate(line)) for line in table]
        code = lines[TILES - 1]
        for c in range(TILES - 2, -1, -1):
            code = jnp.where(chip == c, lines[c], code)
        return code

    order = by_chip(ORDER)
    ready = by_chip([[max(line.index(n) for n in range(t + 1)) for t in range(TILES)] for line in ORDER])

    def device(r, p):
        return {"seq": 2 * r + p // 4, "head": lax.rem(p, 4)}

    def peer(i, sign):
        j = i // 2
        step = 3 if j == 2 else 2 if j == 3 else j
        return lax.rem(chip + 4 + sign * step, 4) * 2 + lax.rem(core + i % 2, 2)

    def source(i):
        return lax.rem(chip + i // 2, 4) * 2 + lax.rem(core + lax.rem(i, 2), 2)

    def remote(src, dst, send, recv, r, p):
        return pltpu.make_async_remote_copy(
            src_ref=src, dst_ref=dst, send_sem=send, recv_sem=recv,
            device_id=device(r, p), device_id_type=MESH,
        )

    barrier = pltpu.get_barrier_semaphore()
    for i in range(1, RING):
        pl.semaphore_signal(barrier, inc=1, device_id=device(row, peer(i, 1)), device_id_type=MESH)

    @pl.when(has_prev)
    def _():
        pl.semaphore_signal(barrier, inc=1, device_id=device(row - 1, me), device_id_type=MESH)

    @pl.when(has_next)
    def _():
        pl.semaphore_signal(barrier, inc=1, device_id=device(row + 1, me), device_id_type=MESH)

    pl.semaphore_wait(barrier, RING - 1 + has_prev.astype(jnp.int32) + has_next.astype(jnp.int32))

    def columns(p, width):
        return pl.ds(pl.multiple_of(p * width, width), width)

    for src, width, stage, send, recv, first in (
        (k_in, HD, kst, k_send, k_recv, RING),
        (v_in, HD, vst, v_send, v_recv, RING),
        (q_in, 2 * HD, qst, q_send, q_recv, 0),
        (g_in, 2 * HD, gst, g_send, g_recv, 0),
    ):
        pltpu.make_async_copy(
            src.at[:, columns(me, width)], stage.at[first + me], recv.at[me]
        ).start()
    def spread(pair, offsets):
        for i in offsets:
            for src, width, stage, send, recv, first in pair:
                to = peer(i, 1)
                remote(
                    src.at[:, columns(to, width)], stage.at[first + me],
                    send.at[to], recv.at[me], row, to,
                ).start()

    keys_values = ((k_in, HD, kst, k_send, k_recv, RING), (v_in, HD, vst, v_send, v_recv, RING))
    queries = ((q_in, 2 * HD, qst, q_send, q_recv, 0), (g_in, 2 * HD, gst, g_send, g_recv, 0))
    spread(keys_values, range(1, RING))

    dkacc[...] = jnp.zeros_like(dkacc)
    dvacc[...] = jnp.zeros_like(dvacc)

    def landed(ref, sem):
        pltpu.make_async_copy(ref, ref, sem).wait()

    def prepare(block):
        at = pl.ds(pl.multiple_of(block * TOK, TOK), TOK)
        key = kst[block]
        high, low = halves(key)
        k4[at, :] = jnp.concatenate([high, low, high, low], axis=1)
        high, low = halves(key.T)
        kt[:, at] = jnp.concatenate([high, low], axis=0)
        high, low = halves(vst[block])
        v4[at, :] = jnp.concatenate([high, low, high, low], axis=1)

    def own_block(i, carry):
        p = source(i)
        landed(kst.at[RING + p], k_recv.at[p])
        landed(vst.at[RING + p], v_recv.at[p])

        @pl.when(has_next)
        def _():
            remote(kst.at[RING + p], kst.at[p], pk_send.at[p], pk_recv.at[p], row + 1, me).start()
            remote(vst.at[RING + p], vst.at[p], pv_send.at[p], pv_recv.at[p], row + 1, me).start()

        prepare(RING + p)
        return carry

    lax.fori_loop(0, 4, own_block, 0)
    spread(queries, range(1, 6))

    @pl.when(chip == 0)
    def _():
        spread(queries, range(6, RING))

    lax.fori_loop(4, RING, own_block, 0)

    def prev_blocks(first, last):
        def prev_block(i, carry):
            p = source(i)
            landed(kst.at[p], pk_recv.at[p])
            landed(vst.at[p], pv_recv.at[p])
            prepare(p)
            return carry

        @pl.when(has_prev)
        def _():
            lax.fori_loop(first, last, prev_block, 0)

    early = RING - 2 * chip
    prev_blocks(0, early)

    @pl.when(chip != 0)
    def _():
        spread(queries, range(6, RING))

    @pl.when(jnp.logical_not(has_prev))
    def _():
        k4[: RING * TOK, :] = jnp.zeros((RING * TOK, 4 * HD), bf16)
        v4[: RING * TOK, :] = jnp.zeros((RING * TOK, 4 * HD), bf16)
        kt[:, : RING * TOK] = jnp.zeros((2 * HD, RING * TOK), bf16)

    lanes = 2 * TILE

    def query_tile(b):
        for e in range(2):
            landed(qst.at[2 * b + e], q_recv.at[2 * b + e])
            landed(gst.at[2 * b + e], g_recv.at[2 * b + e])
        for e in range(2):
            for h in range(2):
                at = slice(h * TILE + e * TOK, h * TILE + (e + 1) * TOK)
                at2 = slice(lanes + h * TILE + e * TOK, lanes + h * TILE + (e + 1) * TOK)
                cols = slice(h * HD, (h + 1) * HD)
                high, low = halves(qst[2 * b + e, :, cols] * (score_scale * LOG2E))
                q4[at, :] = jnp.concatenate([high, high, low, low], axis=1)
                both = jnp.concatenate([high, low], axis=1)
                q2[at, :] = both
                q2[at2, :] = both
                high, low = halves(gst[2 * b + e, :, cols])
                g4[at, :] = jnp.concatenate([high, high, low, low], axis=1)
                both = jnp.concatenate([high, low], axis=1)
                g2[at, :] = both
                g2[at2, :] = both

        def keys(j):
            return pl.ds(pl.multiple_of((b + j) * TILE, TILE), TILE)

        top = jnp.full((8, lanes), -1e30, f32)
        for j in range(SPAN):
            score = dot_nt(k4[keys(j), :], q4[...])
            if j in (0, SPAN - 1):
                key = lax.broadcasted_iota(jnp.int32, (TILE, lanes), 0)
                query = lax.broadcasted_iota(jnp.int32, (TILE, lanes), 1) & (TILE - 1)
                score = jnp.where(key > query if j == 0 else key <= query, score, -1e30)
            if j < SPAN - 1:
                absent = jnp.logical_and(jnp.logical_not(has_prev), b + j < TILES)
                score = score + jnp.where(absent, -1e30, 0.0)
            sbuf[j * TILE : (j + 1) * TILE, :] = score
            top = jnp.maximum(top, jnp.max(score.reshape(TILE // 8, 8, lanes), axis=0))
            pbuf[j * TILE : (j + 1) * TILE, :] = dot_nt(v4[keys(j), :], g4[...])
        top = jnp.max(top, axis=0, keepdims=True)
        total = jnp.zeros((8, lanes), f32)
        inner = jnp.zeros((8, lanes), f32)
        for n in range(SPAN * TILE // CHUNK):
            at = slice(n * CHUNK, (n + 1) * CHUNK)
            raised = jnp.exp2(sbuf[at, :] - top)
            sbuf[at, :] = raised
            total = total + jnp.sum(raised.reshape(CHUNK // 8, 8, lanes), axis=0)
            inner = inner + jnp.sum((raised * pbuf[at, :]).reshape(CHUNK // 8, 8, lanes), axis=0)
        inverse = 1.0 / jnp.sum(total, axis=0, keepdims=True)
        inner = jnp.sum(inner, axis=0, keepdims=True) * inverse
        turned = jnp.zeros((2 * HD, lanes), f32)
        for j in range(SPAN):
            for n in range(TILE // CHUNK):
                at = slice(j * TILE + n * CHUNK, j * TILE + (n + 1) * CHUNK)
                to = slice(n * CHUNK, (n + 1) * CHUNK)
                weight = sbuf[at, :] * inverse
                slope = weight * (pbuf[at, :] - inner)
                high, low = halves(weight)
                wcat[j % 2, to, :lanes] = high
                wcat[j % 2, to, lanes:] = low
                high, low = halves(slope)
                scat[j % 2, to, :lanes] = high
                scat[j % 2, to, lanes:] = low
            part = dot_nn(wcat[j % 2], g2[...])
            dvacc[keys(j), :] += part[:, :HD] + part[:, HD:]
            part = dot_nn(scat[j % 2], q2[...])
            dkacc[keys(j), :] += part[:, :HD] + part[:, HD:]
            turned = turned + dot_nn(kt[:, keys(j)], scat[j % 2, :, :lanes])
            turned = turned + dot_nn(kt[:, keys(j)], scat[j % 2, :, lanes:])
        grad = (turned[:HD] + turned[HD:]) * score_scale
        for e in range(2):
            to = 2 * b + e
            for h in range(2):
                part = grad[:, h * TILE + e * TOK : h * TILE + (e + 1) * TOK]
                dqst[to, :, h * HD : (h + 1) * HD] = part.T

            @pl.when(to == me)
            def _():
                pltpu.make_async_copy(dqst.at[to], dq_out.at[:, columns(me, 2 * HD)], dq_recv.at[me]).start()

            @pl.when(to != me)
            def _():
                remote(
                    dqst.at[to], dq_out.at[:, columns(me, 2 * HD)],
                    dq_send.at[to], dq_recv.at[me], row, to,
                ).start()

    def block_rows(p):
        return pl.ds(pl.multiple_of(p * TOK, TOK), TOK)

    def send_back(t):
        @pl.when(has_prev)
        def _():
            for p in (2 * t, 2 * t + 1):
                remote(dkacc.at[block_rows(p)], hk.at[p], hk_send.at[p], hk_recv.at[p], row - 1, me).start()
                remote(dvacc.at[block_rows(p)], hv.at[p], hv_send.at[p], hv_recv.at[p], row - 1, me).start()

    def step(i, carry):
        b = (order >> (2 * i)) & 3

        @pl.when(i == 1)
        def _():
            prev_blocks(early, RING)

        query_tile(b)
        for t in range(TILES):
            @pl.when(i == (ready >> (2 * t)) & 3)
            def _():
                send_back(t)
        return carry

    lax.fori_loop(0, TILES, step, 0)

    def finish(to, carry):
        @pl.when(has_next)
        def _():
            landed(hk.at[to], hk_recv.at[to])
            landed(hv.at[to], hv_recv.at[to])

        @pl.when(jnp.logical_not(has_next))
        def _():
            hk[to] = jnp.zeros((TOK, HD), f32)
            hv[to] = jnp.zeros((TOK, HD), f32)

        own = block_rows(RING + to)
        dkf[to] = (dkacc[own, :] + hk[to]) * LN2
        dvf[to] = dvacc[own, :] + hv[to]

        @pl.when(to == me)
        def _():
            pltpu.make_async_copy(dkf.at[to], dk_out.at[:, columns(me, HD)], dk_recv.at[me]).start()
            pltpu.make_async_copy(dvf.at[to], dv_out.at[:, columns(me, HD)], dv_recv.at[me]).start()

        @pl.when(to != me)
        def _():
            remote(dkf.at[to], dk_out.at[:, columns(me, HD)], dk_send.at[to], dk_recv.at[me], row, to).start()
            remote(dvf.at[to], dv_out.at[:, columns(me, HD)], dv_send.at[to], dv_recv.at[me], row, to).start()

        return carry

    lax.fori_loop(0, RING, finish, 0)

    def sent(p, carry):
        @pl.when(p != me)
        def _():
            landed(kst.at[RING + me], k_send.at[p])
            landed(vst.at[RING + me], v_send.at[p])
            landed(qst.at[me], q_send.at[p])
            landed(gst.at[me], g_send.at[p])
            landed(dqst.at[p], dq_send.at[p])
            landed(dkf.at[p], dk_send.at[p])
            landed(dvf.at[p], dv_send.at[p])

        @pl.when(has_next)
        def _():
            landed(kst.at[RING + p], pk_send.at[p])
            landed(vst.at[RING + p], pv_send.at[p])

        return carry

    lax.fori_loop(0, RING, sent, 0)

    @pl.when(has_prev)
    def _():
        def halo_sent(p, carry):
            landed(dkacc.at[block_rows(p)], hk_send.at[p])
            landed(dvacc.at[block_rows(p)], hv_send.at[p])
            return carry

        lax.fori_loop(0, RING, halo_sent, 0)

    def got(p, carry):
        landed(dq_out.at[:, columns(p, 2 * HD)], dq_recv.at[p])
        landed(dk_out.at[:, columns(p, HD)], dk_recv.at[p])
        landed(dv_out.at[:, columns(p, HD)], dv_recv.at[p])
        return carry

    lax.fori_loop(0, RING, got, 0)


def solution(mesh):
    rows = mesh.shape["seq"] // 2

    def per_device(query, key_in, value_in, d_out):
        lanes = 2 * TILE
        all_keys = 2 * RING * TOK
        dma = pltpu.SemaphoreType.DMA
        return pl.pallas_call(
            lambda *refs: kernel(rows, *refs),
            out_shape=(
                jax.ShapeDtypeStruct(query.shape, f32),
                jax.ShapeDtypeStruct(key_in.shape, f32),
                jax.ShapeDtypeStruct(value_in.shape, f32),
            ),
            in_specs=[pl.BlockSpec(memory_space=pl.ANY)] * 4,
            out_specs=[pl.BlockSpec(memory_space=pl.ANY)] * 3,
            scratch_shapes=[
                pltpu.VMEM((2 * RING, TOK, HD), f32),
                pltpu.VMEM((2 * RING, TOK, HD), f32),
                pltpu.VMEM((RING, TOK, 2 * HD), f32),
                pltpu.VMEM((RING, TOK, 2 * HD), f32),
                pltpu.VMEM((all_keys, 4 * HD), bf16),
                pltpu.VMEM((all_keys, 4 * HD), bf16),
                pltpu.VMEM((2 * HD, all_keys), bf16),
                pltpu.VMEM((lanes, 4 * HD), bf16),
                pltpu.VMEM((2 * lanes, 2 * HD), bf16),
                pltpu.VMEM((lanes, 4 * HD), bf16),
                pltpu.VMEM((2 * lanes, 2 * HD), bf16),
                pltpu.VMEM((SPAN * TILE, lanes), f32),
                pltpu.VMEM((SPAN * TILE, lanes), f32),
                pltpu.VMEM((2, TILE, 2 * lanes), bf16),
                pltpu.VMEM((2, TILE, 2 * lanes), bf16),
                pltpu.VMEM((all_keys, HD), f32),
                pltpu.VMEM((all_keys, HD), f32),
                pltpu.VMEM((RING, TOK, 2 * HD), f32),
                pltpu.VMEM((RING, TOK, HD), f32),
                pltpu.VMEM((RING, TOK, HD), f32),
                pltpu.VMEM((RING, TOK, HD), f32),
                pltpu.VMEM((RING, TOK, HD), f32),
            ]
            + [dma((RING,))] * 22,
            compiler_params=pltpu.CompilerParams(
                collective_id=0, has_side_effects=True, vmem_limit_bytes=60 * 2**20
            ),
            cost_estimate=pl.CostEstimate(
                flops=5 * 2 * 2 * 1024 * 1280 * HD, bytes_accessed=6 * 2**20, transcendentals=2 * 1024 * 1280
            ),
        )(query, key_in, value_in, d_out)

    spec = P(("seq", "head"), None)
    return jax.shard_map(
        per_device, mesh=mesh, in_specs=(spec,) * 4, out_specs=(spec,) * 3, check_vma=False
    )
```

```python
import math

import jax
import jax.numpy as jnp
from jax import lax
from jax.experimental import pallas as pl
from jax.experimental.pallas import tpu as pltpu
from jax.sharding import PartitionSpec as P

HD = 128
TOK = 128
RING = 8
TILE = 256
TILES = 4
SPAN = TILES + 1
CHUNK = 64
LOG2E = math.log2(math.e)
LN2 = math.log(2.0)
ORDER = ((0, 1, 3, 2), (1, 0, 2, 3), (2, 3, 0, 1), (3, 0, 2, 1))
score_scale = 168.0 ** (-0.5)
MESH = pl.DeviceIdType.MESH
f32 = jnp.float32
bf16 = jnp.bfloat16


def halves(value):
    high = value.astype(bf16)
    low = (value - high.astype(f32)).astype(bf16)
    return high, low


def dot_nt(a, b):
    return lax.dot_general(a, b, (((1,), (1,)), ((), ())), preferred_element_type=f32)


def dot_nn(a, b):
    return lax.dot_general(a, b, (((1,), (0,)), ((), ())), preferred_element_type=f32)


def kernel(
    rows,
    q_in, k_in, v_in, g_in,
    dq_out, dk_out, dv_out,
    kst, vst, qst, gst,
    k4, v4, kt, q4, q2, g4, g2,
    sbuf, pbuf, wcat, scat,
    dkacc, dvacc, dqst, hk, hv, dkf, dvf,
    k_send, k_recv, v_send, v_recv, q_send, q_recv, g_send, g_recv,
    pk_send, pk_recv, pv_send, pv_recv,
    hk_send, hk_recv, hv_send, hv_recv,
    dq_send, dq_recv, dk_send, dk_recv, dv_send, dv_recv,
):
    seq = lax.axis_index("seq")
    head = lax.axis_index("head")
    row = seq // 2
    me = lax.rem(seq, 2) * 4 + head
    chip = me // 2
    core = lax.rem(me, 2)
    has_prev = row > 0
    has_next = row < rows - 1

    def by_chip(table):
        lines = [sum(n << (2 * k) for k, n in enumerate(line)) for line in table]
        code = lines[TILES - 1]
        for c in range(TILES - 2, -1, -1):
            code = jnp.where(chip == c, lines[c], code)
        return code

    order = by_chip(ORDER)
    ready = by_chip([[max(line.index(n) for n in range(t + 1)) for t in range(TILES)] for line in ORDER])

    def device(r, p):
        return {"seq": 2 * r + p // 4, "head": lax.rem(p, 4)}

    def peer(i, sign):
        j = i // 2
        step = 3 if j == 2 else 2 if j == 3 else j
        return lax.rem(chip + 4 + sign * step, 4) * 2 + lax.rem(core + i % 2, 2)

    def source(i):
        return lax.rem(chip + i // 2, 4) * 2 + lax.rem(core + lax.rem(i, 2), 2)

    def remote(src, dst, send, recv, r, p):
        return pltpu.make_async_remote_copy(
            src_ref=src, dst_ref=dst, send_sem=send, recv_sem=recv,
            device_id=device(r, p), device_id_type=MESH,
        )

    barrier = pltpu.get_barrier_semaphore()
    for i in range(1, RING):
        pl.semaphore_signal(barrier, inc=1, device_id=device(row, peer(i, 1)), device_id_type=MESH)

    @pl.when(has_prev)
    def _():
        pl.semaphore_signal(barrier, inc=1, device_id=device(row - 1, me), device_id_type=MESH)

    @pl.when(has_next)
    def _():
        pl.semaphore_signal(barrier, inc=1, device_id=device(row + 1, me), device_id_type=MESH)

    pl.semaphore_wait(barrier, RING - 1 + has_prev.astype(jnp.int32) + has_next.astype(jnp.int32))

    def columns(p, width):
        return pl.ds(pl.multiple_of(p * width, width), width)

    for src, width, stage, send, recv, first in (
        (k_in, HD, kst, k_send, k_recv, RING),
        (v_in, HD, vst, v_send, v_recv, RING),
        (q_in, 2 * HD, qst, q_send, q_recv, 0),
        (g_in, 2 * HD, gst, g_send, g_recv, 0),
    ):
        pltpu.make_async_copy(
            src.at[:, columns(me, width)], stage.at[first + me], recv.at[me]
        ).start()
    def spread(pair, offsets):
        for i in offsets:
            for src, width, stage, send, recv, first in pair:
                to = peer(i, 1)
                remote(
                    src.at[:, columns(to, width)], stage.at[first + me],
                    send.at[to], recv.at[me], row, to,
                ).start()

    keys_values = ((k_in, HD, kst, k_send, k_recv, RING), (v_in, HD, vst, v_send, v_recv, RING))
    queries = ((q_in, 2 * HD, qst, q_send, q_recv, 0), (g_in, 2 * HD, gst, g_send, g_recv, 0))
    spread(keys_values, range(1, RING))

    @pl.when(chip == 0)
    def _():
        spread(queries, range(1, RING))


    dkacc[...] = jnp.zeros_like(dkacc)
    dvacc[...] = jnp.zeros_like(dvacc)

    def landed(ref, sem):
        pltpu.make_async_copy(ref, ref, sem).wait()

    def prepare(block):
        at = pl.ds(pl.multiple_of(block * TOK, TOK), TOK)
        key = kst[block]
        high, low = halves(key)
        k4[at, :] = jnp.concatenate([high, low, high, low], axis=1)
        high, low = halves(key.T)
        kt[:, at] = jnp.concatenate([high, low], axis=0)
        high, low = halves(vst[block])
        v4[at, :] = jnp.concatenate([high, low, high, low], axis=1)

    def own_block(i, carry):
        p = source(i)
        landed(kst.at[RING + p], k_recv.at[p])
        landed(vst.at[RING + p], v_recv.at[p])

        @pl.when(has_next)
        def _():
            remote(kst.at[RING + p], kst.at[p], pk_send.at[p], pk_recv.at[p], row + 1, me).start()
            remote(vst.at[RING + p], vst.at[p], pv_send.at[p], pv_recv.at[p], row + 1, me).start()

        prepare(RING + p)
        return carry

    lax.fori_loop(0, 4, own_block, 0)

    @pl.when(chip != 0)
    def _():
        spread(queries, range(1, 6))

    lax.fori_loop(4, RING, own_block, 0)

    def prev_blocks(first, last):
        def prev_block(i, carry):
            p = source(i)
            landed(kst.at[p], pk_recv.at[p])
            landed(vst.at[p], pv_recv.at[p])
            prepare(p)
            return carry

        @pl.when(has_prev)
        def _():
            lax.fori_loop(first, last, prev_block, 0)

    early = RING - 2 * chip
    prev_blocks(0, early)

    @pl.when(chip != 0)
    def _():
        spread(queries, range(6, RING))

    @pl.when(jnp.logical_not(has_prev))
    def _():
        k4[: RING * TOK, :] = jnp.zeros((RING * TOK, 4 * HD), bf16)
        v4[: RING * TOK, :] = jnp.zeros((RING * TOK, 4 * HD), bf16)
        kt[:, : RING * TOK] = jnp.zeros((2 * HD, RING * TOK), bf16)

    def block_rows(p):
        return pl.ds(pl.multiple_of(p * TOK, TOK), TOK)

    def send_back(t):
        @pl.when(has_prev)
        def _():
            for p in (2 * t, 2 * t + 1):
                remote(dkacc.at[block_rows(p)], hk.at[p], hk_send.at[p], hk_recv.at[p], row - 1, me).start()
                remote(dvacc.at[block_rows(p)], hv.at[p], hv_send.at[p], hv_recv.at[p], row - 1, me).start()

    lanes = 2 * TILE

    def query_tile(b, i):
        for e in range(2):
            landed(qst.at[2 * b + e], q_recv.at[2 * b + e])
            landed(gst.at[2 * b + e], g_recv.at[2 * b + e])
        for e in range(2):
            for h in range(2):
                at = slice(h * TILE + e * TOK, h * TILE + (e + 1) * TOK)
                at2 = slice(lanes + h * TILE + e * TOK, lanes + h * TILE + (e + 1) * TOK)
                cols = slice(h * HD, (h + 1) * HD)
                high, low = halves(qst[2 * b + e, :, cols] * (score_scale * LOG2E))
                q4[at, :] = jnp.concatenate([high, high, low, low], axis=1)
                both = jnp.concatenate([high, low], axis=1)
                q2[at, :] = both
                q2[at2, :] = both
                high, low = halves(gst[2 * b + e, :, cols])
                g4[at, :] = jnp.concatenate([high, high, low, low], axis=1)
                both = jnp.concatenate([high, low], axis=1)
                g2[at, :] = both
                g2[at2, :] = both

        def keys(j):
            return pl.ds(pl.multiple_of((b + j) * TILE, TILE), TILE)

        top = jnp.full((8, lanes), -1e30, f32)
        for j in range(SPAN):
            score = dot_nt(k4[keys(j), :], q4[...])
            if j in (0, SPAN - 1):
                key = lax.broadcasted_iota(jnp.int32, (TILE, lanes), 0)
                query = lax.broadcasted_iota(jnp.int32, (TILE, lanes), 1) & (TILE - 1)
                score = jnp.where(key > query if j == 0 else key <= query, score, -1e30)
            if j < SPAN - 1:
                absent = jnp.logical_and(jnp.logical_not(has_prev), b + j < TILES)
                score = score + jnp.where(absent, -1e30, 0.0)
            sbuf[j * TILE : (j + 1) * TILE, :] = score
            top = jnp.maximum(top, jnp.max(score.reshape(TILE // 8, 8, lanes), axis=0))
            pbuf[j * TILE : (j + 1) * TILE, :] = dot_nt(v4[keys(j), :], g4[...])
        top = jnp.max(top, axis=0, keepdims=True)
        total = jnp.zeros((8, lanes), f32)
        inner = jnp.zeros((8, lanes), f32)
        for n in range(SPAN * TILE // CHUNK):
            at = slice(n * CHUNK, (n + 1) * CHUNK)
            raised = jnp.exp2(sbuf[at, :] - top)
            sbuf[at, :] = raised
            total = total + jnp.sum(raised.reshape(CHUNK // 8, 8, lanes), axis=0)
            inner = inner + jnp.sum((raised * pbuf[at, :]).reshape(CHUNK // 8, 8, lanes), axis=0)
        inverse = 1.0 / jnp.sum(total, axis=0, keepdims=True)
        inner = jnp.sum(inner, axis=0, keepdims=True) * inverse
        turned = jnp.zeros((2 * HD, lanes), f32)
        for j in range(SPAN):
            for n in range(TILE // CHUNK):
                at = slice(j * TILE + n * CHUNK, j * TILE + (n + 1) * CHUNK)
                to = slice(n * CHUNK, (n + 1) * CHUNK)
                weight = sbuf[at, :] * inverse
                slope = weight * (pbuf[at, :] - inner)
                high, low = halves(weight)
                wcat[j % 2, to, :lanes] = high
                wcat[j % 2, to, lanes:] = low
                high, low = halves(slope)
                scat[j % 2, to, :lanes] = high
                scat[j % 2, to, lanes:] = low
            part = dot_nn(wcat[j % 2], g2[...])
            dvacc[keys(j), :] += part[:, :HD] + part[:, HD:]
            part = dot_nn(scat[j % 2], q2[...])
            dkacc[keys(j), :] += part[:, :HD] + part[:, HD:]
            if j == 0:
                @pl.when(i == (ready >> (2 * b)) & 3)
                def _():
                    send_back(b)

            turned = turned + dot_nn(kt[:, keys(j)], scat[j % 2, :, :lanes])
            turned = turned + dot_nn(kt[:, keys(j)], scat[j % 2, :, lanes:])
        grad = (turned[:HD] + turned[HD:]) * score_scale
        for e in range(2):
            to = 2 * b + e
            for h in range(2):
                part = grad[:, h * TILE + e * TOK : h * TILE + (e + 1) * TOK]
                dqst[to, :, h * HD : (h + 1) * HD] = part.T

            @pl.when(to == me)
            def _():
                pltpu.make_async_copy(dqst.at[to], dq_out.at[:, columns(me, 2 * HD)], dq_recv.at[me]).start()

            @pl.when(to != me)
            def _():
                remote(
                    dqst.at[to], dq_out.at[:, columns(me, 2 * HD)],
                    dq_send.at[to], dq_recv.at[me], row, to,
                ).start()

    def step(i, carry):
        b = (order >> (2 * i)) & 3

        @pl.when(i == 1)
        def _():
            prev_blocks(early, RING)

        query_tile(b, i)
        for t in range(TILES):
            @pl.when(jnp.logical_and(t != b, i == (ready >> (2 * t)) & 3))
            def _():
                send_back(t)
        return carry

    lax.fori_loop(0, TILES, step, 0)

    def finish(to, carry):
        @pl.when(has_next)
        def _():
            landed(hk.at[to], hk_recv.at[to])
            landed(hv.at[to], hv_recv.at[to])

        @pl.when(jnp.logical_not(has_next))
        def _():
            hk[to] = jnp.zeros((TOK, HD), f32)
            hv[to] = jnp.zeros((TOK, HD), f32)

        own = block_rows(RING + to)
        dkf[to] = (dkacc[own, :] + hk[to]) * LN2
        dvf[to] = dvacc[own, :] + hv[to]

        @pl.when(to == me)
        def _():
            pltpu.make_async_copy(dkf.at[to], dk_out.at[:, columns(me, HD)], dk_recv.at[me]).start()
            pltpu.make_async_copy(dvf.at[to], dv_out.at[:, columns(me, HD)], dv_recv.at[me]).start()

        @pl.when(to != me)
        def _():
            remote(dkf.at[to], dk_out.at[:, columns(me, HD)], dk_send.at[to], dk_recv.at[me], row, to).start()
            remote(dvf.at[to], dv_out.at[:, columns(me, HD)], dv_send.at[to], dv_recv.at[me], row, to).start()

        return carry

    lax.fori_loop(0, RING, finish, 0)

    def sent(p, carry):
        @pl.when(p != me)
        def _():
            landed(kst.at[RING + me], k_send.at[p])
            landed(vst.at[RING + me], v_send.at[p])
            landed(qst.at[me], q_send.at[p])
            landed(gst.at[me], g_send.at[p])
            landed(dqst.at[p], dq_send.at[p])
            landed(dkf.at[p], dk_send.at[p])
            landed(dvf.at[p], dv_send.at[p])

        @pl.when(has_next)
        def _():
            landed(kst.at[RING + p], pk_send.at[p])
            landed(vst.at[RING + p], pv_send.at[p])

        return carry

    lax.fori_loop(0, RING, sent, 0)

    @pl.when(has_prev)
    def _():
        def halo_sent(p, carry):
            landed(dkacc.at[block_rows(p)], hk_send.at[p])
            landed(dvacc.at[block_rows(p)], hv_send.at[p])
            return carry

        lax.fori_loop(0, RING, halo_sent, 0)

    def got(p, carry):
        landed(dq_out.at[:, columns(p, 2 * HD)], dq_recv.at[p])
        landed(dk_out.at[:, columns(p, HD)], dk_recv.at[p])
        landed(dv_out.at[:, columns(p, HD)], dv_recv.at[p])
        return carry

    lax.fori_loop(0, RING, got, 0)


def solution(mesh):
    rows = mesh.shape["seq"] // 2

    def per_device(query, key_in, value_in, d_out):
        lanes = 2 * TILE
        all_keys = 2 * RING * TOK
        dma = pltpu.SemaphoreType.DMA
        return pl.pallas_call(
            lambda *refs: kernel(rows, *refs),
            out_shape=(
                jax.ShapeDtypeStruct(query.shape, f32),
                jax.ShapeDtypeStruct(key_in.shape, f32),
                jax.ShapeDtypeStruct(value_in.shape, f32),
            ),
            in_specs=[pl.BlockSpec(memory_space=pl.ANY)] * 4,
            out_specs=[pl.BlockSpec(memory_space=pl.ANY)] * 3,
            scratch_shapes=[
                pltpu.VMEM((2 * RING, TOK, HD), f32),
                pltpu.VMEM((2 * RING, TOK, HD), f32),
                pltpu.VMEM((RING, TOK, 2 * HD), f32),
                pltpu.VMEM((RING, TOK, 2 * HD), f32),
                pltpu.VMEM((all_keys, 4 * HD), bf16),
                pltpu.VMEM((all_keys, 4 * HD), bf16),
                pltpu.VMEM((2 * HD, all_keys), bf16),
                pltpu.VMEM((lanes, 4 * HD), bf16),
                pltpu.VMEM((2 * lanes, 2 * HD), bf16),
                pltpu.VMEM((lanes, 4 * HD), bf16),
                pltpu.VMEM((2 * lanes, 2 * HD), bf16),
                pltpu.VMEM((SPAN * TILE, lanes), f32),
                pltpu.VMEM((SPAN * TILE, lanes), f32),
                pltpu.VMEM((2, TILE, 2 * lanes), bf16),
                pltpu.VMEM((2, TILE, 2 * lanes), bf16),
                pltpu.VMEM((all_keys, HD), f32),
                pltpu.VMEM((all_keys, HD), f32),
                pltpu.VMEM((RING, TOK, 2 * HD), f32),
                pltpu.VMEM((RING, TOK, HD), f32),
                pltpu.VMEM((RING, TOK, HD), f32),
                pltpu.VMEM((RING, TOK, HD), f32),
                pltpu.VMEM((RING, TOK, HD), f32),
            ]
            + [dma((RING,))] * 22,
            compiler_params=pltpu.CompilerParams(
                collective_id=0, has_side_effects=True, vmem_limit_bytes=60 * 2**20
            ),
            cost_estimate=pl.CostEstimate(
                flops=5 * 2 * 2 * 1024 * 1280 * HD, bytes_accessed=6 * 2**20, transcendentals=2 * 1024 * 1280
            ),
        )(query, key_in, value_in, d_out)

    spec = P(("seq", "head"), None)
    return jax.shard_map(
        per_device, mesh=mesh, in_specs=(spec,) * 4, out_specs=(spec,) * 3, check_vma=False
    )
```

```python
import math

import jax
import jax.numpy as jnp
from jax import lax
from jax.experimental import pallas as pl
from jax.experimental.pallas import tpu as pltpu
from jax.sharding import PartitionSpec as P

HD = 128
TOK = 128
RING = 8
TILE = 256
TILES = 4
SPAN = TILES + 1
CHUNK = 64
LOG2E = math.log2(math.e)
LN2 = math.log(2.0)
ORDER = ((0, 1, 3, 2), (1, 0, 2, 3), (2, 3, 0, 1), (3, 2, 0, 1))
score_scale = 168.0 ** (-0.5)
MESH = pl.DeviceIdType.MESH
f32 = jnp.float32
bf16 = jnp.bfloat16


def halves(value):
    high = value.astype(bf16)
    low = (value - high.astype(f32)).astype(bf16)
    return high, low


def dot_nt(a, b):
    return lax.dot_general(a, b, (((1,), (1,)), ((), ())), preferred_element_type=f32)


def dot_nn(a, b):
    return lax.dot_general(a, b, (((1,), (0,)), ((), ())), preferred_element_type=f32)


def kernel(
    rows,
    q_in, k_in, v_in, g_in,
    dq_out, dk_out, dv_out,
    kst, vst, qst, gst,
    k4, v4, kt, q4, q2, g4, g2,
    sbuf, pbuf, wcat, scat,
    dkacc, dvacc, dqst, hk, hv, dkf, dvf,
    k_send, k_recv, v_send, v_recv, q_send, q_recv, g_send, g_recv,
    pk_send, pk_recv, pv_send, pv_recv,
    hk_send, hk_recv, hv_send, hv_recv,
    dq_send, dq_recv, dk_send, dk_recv, dv_send, dv_recv,
):
    seq = lax.axis_index("seq")
    head = lax.axis_index("head")
    row = seq // 2
    me = lax.rem(seq, 2) * 4 + head
    chip = me // 2
    core = lax.rem(me, 2)
    has_prev = row > 0
    has_next = row < rows - 1

    def by_chip(table):
        lines = [sum(n << (2 * k) for k, n in enumerate(line)) for line in table]
        code = lines[TILES - 1]
        for c in range(TILES - 2, -1, -1):
            code = jnp.where(chip == c, lines[c], code)
        return code

    order = by_chip(ORDER)
    ready = by_chip([[max(line.index(n) for n in range(t + 1)) for t in range(TILES)] for line in ORDER])

    def device(r, p):
        return {"seq": 2 * r + p // 4, "head": lax.rem(p, 4)}

    def peer(i, sign):
        j = i // 2
        step = 3 if j == 2 else 2 if j == 3 else j
        return lax.rem(chip + 4 + sign * step, 4) * 2 + lax.rem(core + i % 2, 2)

    def source(i):
        return lax.rem(chip + i // 2, 4) * 2 + lax.rem(core + lax.rem(i, 2), 2)

    def remote(src, dst, send, recv, r, p):
        return pltpu.make_async_remote_copy(
            src_ref=src, dst_ref=dst, send_sem=send, recv_sem=recv,
            device_id=device(r, p), device_id_type=MESH,
        )

    barrier = pltpu.get_barrier_semaphore()
    for i in range(1, RING):
        pl.semaphore_signal(barrier, inc=1, device_id=device(row, peer(i, 1)), device_id_type=MESH)

    @pl.when(has_prev)
    def _():
        pl.semaphore_signal(barrier, inc=1, device_id=device(row - 1, me), device_id_type=MESH)

    @pl.when(has_next)
    def _():
        pl.semaphore_signal(barrier, inc=1, device_id=device(row + 1, me), device_id_type=MESH)

    pl.semaphore_wait(barrier, RING - 1 + has_prev.astype(jnp.int32) + has_next.astype(jnp.int32))

    def columns(p, width):
        return pl.ds(pl.multiple_of(p * width, width), width)

    for src, width, stage, send, recv, first in (
        (k_in, HD, kst, k_send, k_recv, RING),
        (v_in, HD, vst, v_send, v_recv, RING),
        (q_in, 2 * HD, qst, q_send, q_recv, 0),
        (g_in, 2 * HD, gst, g_send, g_recv, 0),
    ):
        pltpu.make_async_copy(
            src.at[:, columns(me, width)], stage.at[first + me], recv.at[me]
        ).start()
    def spread(pair, offsets):
        for i in offsets:
            for src, width, stage, send, recv, first in pair:
                to = peer(i, 1)
                remote(
                    src.at[:, columns(to, width)], stage.at[first + me],
                    send.at[to], recv.at[me], row, to,
                ).start()

    keys_values = ((k_in, HD, kst, k_send, k_recv, RING), (v_in, HD, vst, v_send, v_recv, RING))
    queries = ((q_in, 2 * HD, qst, q_send, q_recv, 0), (g_in, 2 * HD, gst, g_send, g_recv, 0))
    spread(keys_values, range(1, RING))

    @pl.when(chip == 0)
    def _():
        spread(queries, (1, 2, 3, 6, 7, 4, 5))


    dkacc[...] = jnp.zeros_like(dkacc)
    dvacc[...] = jnp.zeros_like(dvacc)

    def landed(ref, sem):
        pltpu.make_async_copy(ref, ref, sem).wait()

    def prepare(block):
        at = pl.ds(pl.multiple_of(block * TOK, TOK), TOK)
        key = kst[block]
        high, low = halves(key)
        k4[at, :] = jnp.concatenate([high, low, high, low], axis=1)
        high, low = halves(key.T)
        kt[:, at] = jnp.concatenate([high, low], axis=0)
        high, low = halves(vst[block])
        v4[at, :] = jnp.concatenate([high, low, high, low], axis=1)

    def own_block(i, carry):
        p = source(i)
        landed(kst.at[RING + p], k_recv.at[p])
        landed(vst.at[RING + p], v_recv.at[p])

        @pl.when(has_next)
        def _():
            remote(kst.at[RING + p], kst.at[p], pk_send.at[p], pk_recv.at[p], row + 1, me).start()
            remote(vst.at[RING + p], vst.at[p], pv_send.at[p], pv_recv.at[p], row + 1, me).start()

        prepare(RING + p)
        return carry

    lax.fori_loop(0, 4, own_block, 0)

    @pl.when(chip != 0)
    def _():
        spread(queries, range(1, 6))

    lax.fori_loop(4, RING, own_block, 0)

    def prev_blocks(first, last):
        def prev_block(i, carry):
            p = source(i)
            landed(kst.at[p], pk_recv.at[p])
            landed(vst.at[p], pv_recv.at[p])
            prepare(p)
            return carry

        @pl.when(has_prev)
        def _():
            lax.fori_loop(first, last, prev_block, 0)

    early = RING - 2 * chip
    prev_blocks(0, early)

    @pl.when(chip != 0)
    def _():
        spread(queries, range(6, RING))

    @pl.when(jnp.logical_not(has_prev))
    def _():
        k4[: RING * TOK, :] = jnp.zeros((RING * TOK, 4 * HD), bf16)
        v4[: RING * TOK, :] = jnp.zeros((RING * TOK, 4 * HD), bf16)
        kt[:, : RING * TOK] = jnp.zeros((2 * HD, RING * TOK), bf16)

    def block_rows(p):
        return pl.ds(pl.multiple_of(p * TOK, TOK), TOK)

    def send_back(t):
        @pl.when(has_prev)
        def _():
            for p in (2 * t, 2 * t + 1):
                remote(dkacc.at[block_rows(p)], hk.at[p], hk_send.at[p], hk_recv.at[p], row - 1, me).start()
                remote(dvacc.at[block_rows(p)], hv.at[p], hv_send.at[p], hv_recv.at[p], row - 1, me).start()

    lanes = 2 * TILE

    def query_tile(b, i):
        for e in range(2):
            landed(qst.at[2 * b + e], q_recv.at[2 * b + e])
            landed(gst.at[2 * b + e], g_recv.at[2 * b + e])
        for e in range(2):
            for h in range(2):
                at = slice(h * TILE + e * TOK, h * TILE + (e + 1) * TOK)
                at2 = slice(lanes + h * TILE + e * TOK, lanes + h * TILE + (e + 1) * TOK)
                cols = slice(h * HD, (h + 1) * HD)
                high, low = halves(qst[2 * b + e, :, cols] * (score_scale * LOG2E))
                q4[at, :] = jnp.concatenate([high, high, low, low], axis=1)
                both = jnp.concatenate([high, low], axis=1)
                q2[at, :] = both
                q2[at2, :] = both
                high, low = halves(gst[2 * b + e, :, cols])
                g4[at, :] = jnp.concatenate([high, high, low, low], axis=1)
                both = jnp.concatenate([high, low], axis=1)
                g2[at, :] = both
                g2[at2, :] = both

        def keys(j):
            return pl.ds(pl.multiple_of((b + j) * TILE, TILE), TILE)

        top = jnp.full((8, lanes), -1e30, f32)
        for j in range(SPAN):
            score = dot_nt(k4[keys(j), :], q4[...])
            if j in (0, SPAN - 1):
                key = lax.broadcasted_iota(jnp.int32, (TILE, lanes), 0)
                query = lax.broadcasted_iota(jnp.int32, (TILE, lanes), 1) & (TILE - 1)
                score = jnp.where(key > query if j == 0 else key <= query, score, -1e30)
            if j < SPAN - 1:
                absent = jnp.logical_and(jnp.logical_not(has_prev), b + j < TILES)
                score = score + jnp.where(absent, -1e30, 0.0)
            sbuf[j * TILE : (j + 1) * TILE, :] = score
            top = jnp.maximum(top, jnp.max(score.reshape(TILE // 8, 8, lanes), axis=0))
            pbuf[j * TILE : (j + 1) * TILE, :] = dot_nt(v4[keys(j), :], g4[...])
        top = jnp.max(top, axis=0, keepdims=True)
        total = jnp.zeros((8, lanes), f32)
        inner = jnp.zeros((8, lanes), f32)
        for n in range(SPAN * TILE // CHUNK):
            at = slice(n * CHUNK, (n + 1) * CHUNK)
            raised = jnp.exp2(sbuf[at, :] - top)
            sbuf[at, :] = raised
            total = total + jnp.sum(raised.reshape(CHUNK // 8, 8, lanes), axis=0)
            inner = inner + jnp.sum((raised * pbuf[at, :]).reshape(CHUNK // 8, 8, lanes), axis=0)
        inverse = 1.0 / jnp.sum(total, axis=0, keepdims=True)
        inner = jnp.sum(inner, axis=0, keepdims=True) * inverse
        turned = jnp.zeros((2 * HD, lanes), f32)
        for j in range(SPAN):
            for n in range(TILE // CHUNK):
                at = slice(j * TILE + n * CHUNK, j * TILE + (n + 1) * CHUNK)
                to = slice(n * CHUNK, (n + 1) * CHUNK)
                weight = sbuf[at, :] * inverse
                slope = weight * (pbuf[at, :] - inner)
                high, low = halves(weight)
                wcat[j % 2, to, :lanes] = high
                wcat[j % 2, to, lanes:] = low
                high, low = halves(slope)
                scat[j % 2, to, :lanes] = high
                scat[j % 2, to, lanes:] = low
            part = dot_nn(wcat[j % 2], g2[...])
            dvacc[keys(j), :] += part[:, :HD] + part[:, HD:]
            part = dot_nn(scat[j % 2], q2[...])
            dkacc[keys(j), :] += part[:, :HD] + part[:, HD:]
            if j == 0:
                @pl.when(i == (ready >> (2 * b)) & 3)
                def _():
                    send_back(b)

            turned = turned + dot_nn(kt[:, keys(j)], scat[j % 2, :, :lanes])
            turned = turned + dot_nn(kt[:, keys(j)], scat[j % 2, :, lanes:])
        grad = (turned[:HD] + turned[HD:]) * score_scale
        for e in range(2):
            to = 2 * b + e
            for h in range(2):
                part = grad[:, h * TILE + e * TOK : h * TILE + (e + 1) * TOK]
                dqst[to, :, h * HD : (h + 1) * HD] = part.T

            @pl.when(to == me)
            def _():
                pltpu.make_async_copy(dqst.at[to], dq_out.at[:, columns(me, 2 * HD)], dq_recv.at[me]).start()

            @pl.when(to != me)
            def _():
                remote(
                    dqst.at[to], dq_out.at[:, columns(me, 2 * HD)],
                    dq_send.at[to], dq_recv.at[me], row, to,
                ).start()

    def step(i, carry):
        b = (order >> (2 * i)) & 3

        @pl.when(i == 1)
        def _():
            prev_blocks(early, RING)

        query_tile(b, i)
        for t in range(TILES):
            @pl.when(jnp.logical_and(t != b, i == (ready >> (2 * t)) & 3))
            def _():
                send_back(t)
        return carry

    lax.fori_loop(0, TILES, step, 0)

    def finish(to, carry):
        @pl.when(has_next)
        def _():
            landed(hk.at[to], hk_recv.at[to])
            landed(hv.at[to], hv_recv.at[to])

        @pl.when(jnp.logical_not(has_next))
        def _():
            hk[to] = jnp.zeros((TOK, HD), f32)
            hv[to] = jnp.zeros((TOK, HD), f32)

        own = block_rows(RING + to)
        dkf[to] = (dkacc[own, :] + hk[to]) * LN2
        dvf[to] = dvacc[own, :] + hv[to]

        @pl.when(to == me)
        def _():
            pltpu.make_async_copy(dkf.at[to], dk_out.at[:, columns(me, HD)], dk_recv.at[me]).start()
            pltpu.make_async_copy(dvf.at[to], dv_out.at[:, columns(me, HD)], dv_recv.at[me]).start()

        @pl.when(to != me)
        def _():
            remote(dkf.at[to], dk_out.at[:, columns(me, HD)], dk_send.at[to], dk_recv.at[me], row, to).start()
            remote(dvf.at[to], dv_out.at[:, columns(me, HD)], dv_send.at[to], dv_recv.at[me], row, to).start()

        return carry

    lax.fori_loop(0, RING, finish, 0)

    def sent(p, carry):
        @pl.when(p != me)
        def _():
            landed(kst.at[RING + me], k_send.at[p])
            landed(vst.at[RING + me], v_send.at[p])
            landed(qst.at[me], q_send.at[p])
            landed(gst.at[me], g_send.at[p])
            landed(dqst.at[p], dq_send.at[p])
            landed(dkf.at[p], dk_send.at[p])
            landed(dvf.at[p], dv_send.at[p])

        @pl.when(has_next)
        def _():
            landed(kst.at[RING + p], pk_send.at[p])
            landed(vst.at[RING + p], pv_send.at[p])

        return carry

    lax.fori_loop(0, RING, sent, 0)

    @pl.when(has_prev)
    def _():
        def halo_sent(p, carry):
            landed(dkacc.at[block_rows(p)], hk_send.at[p])
            landed(dvacc.at[block_rows(p)], hv_send.at[p])
            return carry

        lax.fori_loop(0, RING, halo_sent, 0)

    def got(p, carry):
        landed(dq_out.at[:, columns(p, 2 * HD)], dq_recv.at[p])
        landed(dk_out.at[:, columns(p, HD)], dk_recv.at[p])
        landed(dv_out.at[:, columns(p, HD)], dv_recv.at[p])
        return carry

    lax.fori_loop(0, RING, got, 0)


def solution(mesh):
    rows = mesh.shape["seq"] // 2

    def per_device(query, key_in, value_in, d_out):
        lanes = 2 * TILE
        all_keys = 2 * RING * TOK
        dma = pltpu.SemaphoreType.DMA
        return pl.pallas_call(
            lambda *refs: kernel(rows, *refs),
            out_shape=(
                jax.ShapeDtypeStruct(query.shape, f32),
                jax.ShapeDtypeStruct(key_in.shape, f32),
                jax.ShapeDtypeStruct(value_in.shape, f32),
            ),
            in_specs=[pl.BlockSpec(memory_space=pl.ANY)] * 4,
            out_specs=[pl.BlockSpec(memory_space=pl.ANY)] * 3,
            scratch_shapes=[
                pltpu.VMEM((2 * RING, TOK, HD), f32),
                pltpu.VMEM((2 * RING, TOK, HD), f32),
                pltpu.VMEM((RING, TOK, 2 * HD), f32),
                pltpu.VMEM((RING, TOK, 2 * HD), f32),
                pltpu.VMEM((all_keys, 4 * HD), bf16),
                pltpu.VMEM((all_keys, 4 * HD), bf16),
                pltpu.VMEM((2 * HD, all_keys), bf16),
                pltpu.VMEM((lanes, 4 * HD), bf16),
                pltpu.VMEM((2 * lanes, 2 * HD), bf16),
                pltpu.VMEM((lanes, 4 * HD), bf16),
                pltpu.VMEM((2 * lanes, 2 * HD), bf16),
                pltpu.VMEM((SPAN * TILE, lanes), f32),
                pltpu.VMEM((SPAN * TILE, lanes), f32),
                pltpu.VMEM((2, TILE, 2 * lanes), bf16),
                pltpu.VMEM((2, TILE, 2 * lanes), bf16),
                pltpu.VMEM((all_keys, HD), f32),
                pltpu.VMEM((all_keys, HD), f32),
                pltpu.VMEM((RING, TOK, 2 * HD), f32),
                pltpu.VMEM((RING, TOK, HD), f32),
                pltpu.VMEM((RING, TOK, HD), f32),
                pltpu.VMEM((RING, TOK, HD), f32),
                pltpu.VMEM((RING, TOK, HD), f32),
            ]
            + [dma((RING,))] * 22,
            compiler_params=pltpu.CompilerParams(
                collective_id=0, has_side_effects=True, vmem_limit_bytes=60 * 2**20
            ),
            cost_estimate=pl.CostEstimate(
                flops=5 * 2 * 2 * 1024 * 1280 * HD, bytes_accessed=6 * 2**20, transcendentals=2 * 1024 * 1280
            ),
        )(query, key_in, value_in, d_out)

    spec = P(("seq", "head"), None)
    return jax.shard_map(
        per_device, mesh=mesh, in_specs=(spec,) * 4, out_specs=(spec,) * 3, check_vma=False
    )
```
